1024 devices in a mesh: dp: 128 (over x, y, z_lo), expert: 8 (over z_hi, core).
Axes of the slice: x: 8, y: 8, z: 8 (z_hi: 4, z_lo: 2; z = z_hi * 2 + z_lo), core: 2. Of those that a mesh axis runs over, the one named last changes fastest.
Arguments:
- grad_out: bfloat16 [131072, 2048], P(('dp', 'expert')), may hold values from -1.5 to 1.5
- expert_ids: int32 [131072, 2], P(('dp', 'expert')), may hold values from 0 to 7, all different within a row; in each aligned block of 128 rows (0 to 127, 128 to 255, ...) at most 40 rows name the same one
- gate_probs: bfloat16 [131072, 2], P(('dp', 'expert')), may hold values from 0.099609375 to 1
- hidden_saved: bfloat16 [8, 128, 8, 40, 768], P('expert', 'dp'), may hold values from -24 to 24
- w_down: bfloat16 [8, 768, 2048], P('expert'), may hold values from -0.21875 to 0.21875
Outputs:
- grad_hidden: bfloat16 [131072, 2, 768], P(('dp', 'expert'))
- grad_gate: bfloat16 [131072, 2], P(('dp', 'expert'))
- weight_grad: float32 [8, 768, 2048], P('expert', 'dp')
The draws below stay inside these ranges and needn't reach their ends.
Inputs may be any that keep to these rules, and one draw needn't show every extreme that they name: `expert_ids`: each token names 2 different experts; among the tokens of one device no expert is named more than 40 times, a bound that some block reaches.
All inputs are finite; a program needn't handle non-finite values.
Results may differ from the reference program's by a relative error of at most 0.0049.
Values may be sent and summed in bfloat16 or wider, within the bound.
A program may use at most 64 MiB of HBM per device.

```python
import math
import jax
import jax.numpy as jnp
import numpy as np
from jax import lax

D = 2048
FF = 768
TOPK = 2
TOK_DEV = 128
EXPERTS = 8
CAP = 40
TOKENS = 131072
N_DP = 128
N_EXPERT = 8


def raised(drawn, own_key, source, target, parts, factor):
    def block_of(dim):
        return (jnp.arange(drawn.shape[dim]) // (drawn.shape[dim] // parts)).reshape((-1,) + (1,) * (drawn.ndim - 1 - dim))

    one_side = jax.random.permutation(own_key, parts)[block_of(target)]
    second = (block_of(target) + parts // 2) % parts
    return jnp.where((block_of(source) == one_side) | (block_of(source) == second), factor * drawn, drawn)


def levels(key, shape, shards, smallest, top_value):
    def one(position, parts):
        steps = jax.random.uniform(jax.random.fold_in(jax.random.fold_in(key, 6), position), (parts,), jnp.float32, smallest / len(shards), top_value / len(shards))
        return jnp.repeat(jnp.exp(steps), shape[position] // parts).reshape((-1,) + (1,) * (len(shape) - position - 1))

    loudness = one(*shards[0])
    for cut in shards[1:]:
        loudness = loudness * one(*cut)
    return loudness


def deal_out(stream_key, own, number, rows, number_of, top, limit, lean):
    ranking = jax.random.permutation(stream_key, number_of)
    heavy_load, common = shares(number_of, rows * top, limit, lean, True), shares(number_of, rows * top, limit, lean, False)
    places = jnp.arange(number_of)

    def named(sizes, rotation):
        used = int((sizes > 0).sum())
        fixed = max(1, used // 4)
        passed = fixed + (places - fixed + rotation * (used - fixed)) % max(1, number_of - fixed)
        return jnp.zeros((number_of,), jnp.int32).at[ranking[jnp.where(places < fixed, places, passed)]].set(jnp.asarray(sizes, jnp.int32))

    sizes = jnp.where(number % 4 == 0, named(heavy_load, number // 4), named(common, number - number // 4 - 1))
    mixed = jax.random.permutation(jax.random.fold_in(own, 3), number_of)
    donor, taker = mixed[0:number_of // 2 * 2:2], mixed[1:number_of // 2 * 2:2]
    slack = jnp.minimum(sizes[donor] - 1, limit - sizes[taker]) // 2
    slack = jnp.where((donor == ranking[0]) | (taker == ranking[0]) | (sizes[taker] == 0), 0, jnp.maximum(slack, 0))
    passed = jax.random.randint(jax.random.fold_in(own, 4), (number_of // 2,), 0, 1 << 20) % (slack + 1)
    sizes = sizes.at[donor].add(-passed).at[taker].add(passed)
    items = jnp.searchsorted(jnp.cumsum(sizes), jnp.arange(rows * top), side="right").astype(jnp.int32)
    table = items.reshape(top, rows).T
    table = table[jax.random.permutation(jax.random.fold_in(own, 1), rows)]
    rotation = jax.random.randint(jax.random.fold_in(own, 2), (rows, 1), 0, top)
    return jnp.take_along_axis(table, (jnp.arange(top)[None, :] + rotation) % top, axis=1)


def shares(amount, total, most, slope, full):
    weights = [(1 << 20) // math.isqrt(grade ** slope) + 1 for grade in range(1, amount + 1)]
    largest = most if full else min(most, max(-(-total // amount), total * weights[0] // sum(weights)))
    least = 1 if total - largest >= amount - 1 else 0
    counts, spare = [largest] + [least] * (amount - 1), total - largest - least * (amount - 1)
    while spare > 0:
        free = [i for i in range(1, amount) if counts[i] < largest] or [i for i in range(1, amount) if counts[i] < most]
        mass, budget = sum([weights[i] for i in free]), spare
        for i in free:
            addition = min(most - counts[i], max(1, budget * weights[i] // mass), spare)
            counts[i] = counts[i] + addition
            spare = spare - addition
    return np.array(counts)


def scatter_about(key, dims, deviation, bound, cuts=(), held_as=jnp.bfloat16):
    entries = jax.random.normal(key, dims, jnp.float32) * deviation
    if len(cuts) > 0:
        entries = levels(key, dims, cuts, -0.22, 0.18) * entries
    return jnp.clip(entries, min=-bound, max=bound).astype(held_as)


def gaussian_with(stream_key, shape, deviation, bound, shards, heavy, kind=jnp.bfloat16):
    values = deviation * jax.random.normal(stream_key, shape, jnp.float32)
    if shards:
        values = values * levels(stream_key, shape, shards, -0.22, 0.18)
    return jnp.clip(raised(values, jax.random.fold_in(stream_key, 3), *heavy), -bound, bound).astype(kind)


def setup_inputs(seed: int = 0) -> dict:
    arg_keys = jax.random.split(jax.random.key(seed), 6)
    grad_out = scatter_about(arg_keys[0], (TOKENS, D), 0.25, 1.5, ((0, 1024),))
    expert_ids_keys = jax.random.split(jax.random.fold_in(arg_keys[1], 1), TOKENS // TOK_DEV)
    expert_ids_turns = jax.random.permutation(jax.random.fold_in(arg_keys[1], 3), TOKENS // TOK_DEV)
    expert_ids = jax.vmap(lambda own, number: deal_out(jax.random.fold_in(arg_keys[1], 2), own, number, TOK_DEV, EXPERTS, TOPK, CAP, 1))(expert_ids_keys, expert_ids_turns).reshape((TOKENS, TOPK))
    gate_probs = jnp.clip(0.099609375 + 0.9003906 * jax.random.uniform(arg_keys[2], (TOKENS, TOPK), jnp.float32) ** levels(arg_keys[2], (TOKENS, TOPK), ((0, 1024),), -0.2, 0.2), 0.099609375, 1.0).astype(jnp.bfloat16)
    hidden_saved = gaussian_with(arg_keys[3], (EXPERTS, N_DP, N_EXPERT, CAP, FF), 1.0, 24.0, ((0, 8), (1, 128)), (1, 4, 128, 5.5))
    w_down = scatter_about(arg_keys[4], (EXPERTS, FF, D), FF ** -0.5, 0.21875, ((0, 8),))
    return dict(grad_out=grad_out, expert_ids=expert_ids, gate_probs=gate_probs, hidden_saved=hidden_saved, w_down=w_down)


def reference(grad_out, expert_ids, gate_probs, hidden_saved, w_down):
    devices = N_DP * N_EXPERT
    routed = TOK_DEV * TOPK
    flat_ids = expert_ids.reshape(devices, routed)
    onehot = (flat_ids[:, :, None] == jnp.arange(EXPERTS, dtype=jnp.int32)[None, None, :]).astype(jnp.int32)
    slot_of = jnp.sum((jnp.cumsum(onehot, axis=1) - 1) * onehot, axis=2).astype(jnp.int32)
    token_rows = grad_out.reshape(devices, TOK_DEV, D)
    gate_rows = gate_probs.reshape(devices, TOK_DEV, TOPK)
    id_rows = expert_ids.reshape(devices, TOK_DEV, TOPK)
    slot_rows = slot_of.reshape(devices, TOK_DEV, TOPK)
    dev_index = jnp.arange(devices, dtype=jnp.int32)[:, None]

    def one_expert(carried, expert):
        hid_out, gate_out = carried
        spot = jnp.where(id_rows == expert, slot_rows, CAP).astype(jnp.int32)
        buffer = jnp.zeros((devices, CAP + 1, D), jnp.bfloat16)
        gate_buf = jnp.zeros((devices, CAP + 1), jnp.bfloat16)
        for pick in range(TOPK):
            buffer = buffer.at[dev_index, spot[:, :, pick]].set(token_rows)
            gate_buf = gate_buf.at[dev_index, spot[:, :, pick]].set(gate_rows[:, :, pick])
        incoming = buffer[:, :CAP].reshape(devices * CAP, D)
        gate_in = gate_buf[:, :CAP].reshape(devices * CAP).astype(jnp.float32)
        saved_rows = lax.dynamic_index_in_dim(hidden_saved, expert, 0, keepdims=False).reshape(devices * CAP, FF)
        weight = lax.dynamic_index_in_dim(w_down, expert, 0, keepdims=False)
        recomputed = jnp.dot(saved_rows, weight, preferred_element_type=jnp.float32)
        gate_grad = jnp.sum(incoming.astype(jnp.float32) * recomputed, axis=1).astype(jnp.bfloat16)
        scaled = (gate_in[:, None] * incoming.astype(jnp.float32)).astype(jnp.bfloat16)
        hidden_grad = jnp.dot(scaled, weight.T, preferred_element_type=jnp.float32).astype(jnp.bfloat16)
        weight_grad = jnp.dot(saved_rows.T, scaled, preferred_element_type=jnp.float32)
        hidden_grad = hidden_grad.reshape(devices, CAP, FF)
        gate_grad = gate_grad.reshape(devices, CAP)
        for pick in range(TOPK):
            chosen = id_rows[:, :, pick] == expert
            place = jnp.minimum(slot_rows[:, :, pick], CAP - 1).astype(jnp.int32)
            values = hidden_grad[dev_index, place]
            hid_out = hid_out.at[:, :, pick].set(jnp.where(chosen[:, :, None], values, hid_out[:, :, pick]))
            gate_vals = gate_grad[dev_index, place]
            gate_out = gate_out.at[:, :, pick].set(jnp.where(chosen, gate_vals, gate_out[:, :, pick]))
        return (hid_out, gate_out), weight_grad

    start_hid = jnp.zeros((devices, TOK_DEV, TOPK, FF), jnp.bfloat16)
    start_gate = jnp.zeros((devices, TOK_DEV, TOPK), jnp.bfloat16)
    (hid_out, gate_out), weight_grad = lax.scan(one_expert, (start_hid, start_gate), jnp.arange(EXPERTS, dtype=jnp.int32))
    return hid_out.reshape(TOKENS, TOPK, FF), gate_out.reshape(TOKENS, TOPK), weight_grad
```

```python
import functools

import jax
import jax.numpy as jnp
from jax import lax
from jax.experimental import pallas as pl
from jax.experimental.pallas import tpu as pltpu
from jax.sharding import PartitionSpec as P

MESH = pl.DeviceIdType.MESH
NX, NY, NZ = 8, 8, 2
NE, CAP, TOK, D, FF = 8, 40, 128, 2048, 768
ROWS = NE * CAP
NC = 8
DC = D // NC
H = DC // 2
FH = FF // 2
WINDOW = 2
LAG1, LAG2, LAG3 = 1, 2, 3
F32, BF16 = jnp.float32, jnp.bfloat16
NT = (((1,), (1,)), ((), ()))


def wait_bytes(ref, sem):
    pltpu.make_async_copy(ref, ref, sem).wait()


def fold(block, width):
    left = block[:, :width].reshape(NE, CAP, width)
    right = block[:, width:].reshape(NE, CAP, width)
    return jnp.concatenate([left, right], axis=1).astype(BF16)


def unfold(block, width):
    block = block.astype(F32)
    left = block[:, :CAP, :].reshape(ROWS, width)
    right = block[:, CAP:, :].reshape(ROWS, width)
    return jnp.concatenate([left, right], axis=1).astype(BF16)


def kernel(
    ids_ref, gate_ref, go_ref, hid_hbm, w_hbm,
    gh_ref, gg_ref, wg_ref,
    hid, w, place, picked, hid_t, send, recv, grad, part, r1, q2, r2, tot, r3,
    back, back_in, gate_out, gate_in,
    local, fwd_s, fwd_r, s1_s, s1_r, s2_s, s2_r, s3_s, s3_r, ret_s, ret_r, gs, gr,
):
    dp = lax.axis_index("dp")
    me = lax.axis_index("expert")
    core = lax.rem(me, 2)
    x, y, zl = dp // (NY * NZ), lax.rem(dp // NZ, NY), lax.rem(dp, NZ)
    first = jnp.where(core == 0, x, y)
    second = jnp.where(core == 0, y, x)

    def peer(k):
        return lax.rem(me + k, NE)

    def along(sx, sy):
        return (lax.rem(x + sx, NX) * NY + lax.rem(y + sy, NY)) * NZ + zl

    def dev1(k):
        return (along(k * (1 - core), k * core), me)

    def dev2(k):
        return (along(k * core, k * (1 - core)), me)

    dev3 = (dp + 1 - 2 * zl, me)

    barrier = pltpu.get_barrier_semaphore()

    def greet(k, _):
        for device in ((dp, peer(k)), dev1(k), dev2(k)):
            pl.semaphore_signal(barrier, inc=1, device_id=device, device_id_type=MESH)
        return 0

    lax.fori_loop(1, 8, greet, 0)
    pl.semaphore_signal(barrier, inc=1, device_id=dev3, device_id_type=MESH)

    load_hid = pltpu.make_async_copy(hid_hbm, hid, local.at[0])
    load_w = pltpu.make_async_copy(w_hbm, w, local.at[1])
    load_hid.start()
    load_w.start()

    ids = ids_ref[...]
    gates = gate_ref[...].astype(F32)
    expert = lax.broadcasted_iota(jnp.int32, (NE, TOK), 0)
    chosen = [ids[k : k + 1] == expert for k in range(2)]
    named = jnp.where(chosen[0] | chosen[1], 1.0, 0.0)
    before = (
        lax.broadcasted_iota(jnp.int32, (TOK, TOK), 0) < lax.broadcasted_iota(jnp.int32, (TOK, TOK), 1)
    )
    slot = jnp.dot(
        named.astype(BF16), jnp.where(before, 1.0, 0.0).astype(BF16), preferred_element_type=F32
    )
    row = lax.broadcasted_iota(jnp.int32, (CAP, TOK), 0).astype(F32)
    spots = []
    for k in range(2):
        own = jnp.where(chosen[k], slot, -1.0)
        spots.append(
            jnp.concatenate(
                [jnp.where(row == own[e : e + 1], 1.0, 0.0) for e in range(NE)], axis=0
            )
        )
    place[...] = (spots[0] * gates[0:1] + spots[1] * gates[1:2]).astype(BF16)

    def dispatch(c):
        columns = go_ref[:, pl.ds(pl.multiple_of(c * DC, DC), DC)]
        rows = jnp.dot(place[...], columns, preferred_element_type=F32)
        send[c] = fold(rows, H)
        recv[c, me] = send[c, me]

    def forward(c):
        def one(k, _):
            pltpu.make_async_remote_copy(
                src_ref=send.at[c, peer(k)], dst_ref=recv.at[c, me],
                send_sem=fwd_s.at[c], recv_sem=fwd_r.at[c],
                device_id=(dp, peer(k)), device_id_type=MESH,
            ).start()
            return 0

        lax.fori_loop(1, NE, one, 0)

    dispatch(0)
    pl.semaphore_wait(barrier, 22)
    forward(0)

    def prepare(c, _):
        dispatch(c)

        @pl.when(c < WINDOW)
        def _():
            forward(c)

        return 0

    lax.fori_loop(1, NC, prepare, 0)

    eye = (
        lax.broadcasted_iota(jnp.int32, (TOK, TOK), 0) == lax.broadcasted_iota(jnp.int32, (TOK, TOK), 1)
    )
    eye = jnp.where(eye, 1.0, 0.0).astype(BF16)
    for k in range(2):
        picked[k] = lax.dot_general(
            eye, spots[k].astype(BF16), NT, preferred_element_type=F32
        ).astype(BF16)

    j = lax.broadcasted_iota(jnp.int32, (FF, 1), 0)
    major = (j * 683) >> 16
    rest = j - 96 * major
    minor = (rest * 171) >> 11
    turned = minor * 96 + major * 12 + (rest - 12 * minor)
    source = jnp.where(core == 0, j, turned)
    order = jnp.where(lax.broadcasted_iota(jnp.int32, (FF, FF), 1) == source, 1.0, 0.0).astype(BF16)
    load_hid.wait()
    hid_t[...] = lax.dot_general(order, hid[...], NT, preferred_element_type=F32).astype(BF16)
    grad[...] = jnp.zeros_like(grad)

    i = lax.broadcasted_iota(jnp.int32, (128, 1), 0)
    inner = i & 7
    origin = (i >> 4) * 12 + ((i >> 3) & 1) * 6 + inner
    spread = lax.broadcasted_iota(jnp.int32, (128, 96), 1) == jnp.where(inner < 6, origin, -1)
    spread = jnp.where(spread, 1.0, 0.0).astype(BF16)
    load_w.wait()

    def step(c, _):
        @pl.when(c < NC)
        def _():
            wait_bytes(recv.at[c, pl.ds(0, NE - 1)], fwd_r.at[c])

            @pl.when(c + WINDOW < NC)
            def _():
                forward(c + WINDOW)

            rows = unfold(recv[c], H)
            part[c] = (
                jnp.dot(hid_t[...], rows, preferred_element_type=F32).astype(BF16).reshape(8, 96, DC)
            )

            def one(k, _):
                pltpu.make_async_remote_copy(
                    src_ref=part.at[c, lax.rem(first + k, 8)], dst_ref=r1.at[c, k - 1],
                    send_sem=s1_s.at[c], recv_sem=s1_r.at[c],
                    device_id=dev1(k), device_id_type=MESH,
                ).start()
                return 0

            lax.fori_loop(1, 8, one, 0)
            columns = w[:, pl.ds(pl.multiple_of(c * DC, DC), DC)]
            grad[...] += lax.dot_general(rows, columns, NT, preferred_element_type=F32)

        @pl.when(c == NC - 1)
        def _():
            total = grad[...]
            gate_sum = jnp.sum(hid[...].astype(F32) * total, axis=1, keepdims=True)
            shape = (NE, CAP, 128)
            diagonal = lax.broadcasted_iota(jnp.int32, shape, 1) == lax.broadcasted_iota(jnp.int32, shape, 2)
            flat = jnp.sum(
                jnp.where(diagonal, gate_sum.reshape(NE, CAP, 1), 0.0), axis=1, keepdims=True
            )
            gate_out[...] = jnp.broadcast_to(flat, (NE, 8, 128))
            back[...] = fold(total, FH)
            back_in[me] = back[me]
            gate_in[me] = gate_out[me]

            def one(k, _):
                pltpu.make_async_remote_copy(
                    src_ref=back.at[peer(k)], dst_ref=back_in.at[me],
                    send_sem=ret_s.at[0], recv_sem=ret_r.at[0],
                    device_id=(dp, peer(k)), device_id_type=MESH,
                ).start()
                pltpu.make_async_remote_copy(
                    src_ref=gate_out.at[peer(k)], dst_ref=gate_in.at[me],
                    send_sem=gs.at[0], recv_sem=gr.at[0],
                    device_id=(dp, peer(k)), device_id_type=MESH,
                ).start()
                return 0

            lax.fori_loop(1, NE, one, 0)

        @pl.when((c >= LAG1) & (c < NC + LAG1))
        def _():
            b = c - LAG1
            wait_bytes(r1.at[b], s1_r.at[b])
            total = part[b, first].astype(F32)
            for k in range(7):
                total += r1[b, k].astype(F32)
            wide = jnp.dot(spread, total.astype(BF16), preferred_element_type=F32)
            q2[b] = wide.astype(BF16).reshape(8, 16, DC)

            def one(k, _):
                pltpu.make_async_remote_copy(
                    src_ref=q2.at[b, lax.rem(second + k, 8)], dst_ref=r2.at[b, k - 1],
                    send_sem=s2_s.at[b], recv_sem=s2_r.at[b],
                    device_id=dev2(k), device_id_type=MESH,
                ).start()
                return 0

            lax.fori_loop(1, 8, one, 0)

        @pl.when((c >= LAG2) & (c < NC + LAG2))
        def _():
            b = c - LAG2
            wait_bytes(r2.at[b], s2_r.at[b])
            total = q2[b, second].astype(F32)
            for k in range(7):
                total += r2[b, k].astype(F32)
            tot[b] = total.reshape(2, 8, DC)
            pltpu.make_async_remote_copy(
                src_ref=tot.at[b, 1 - zl], dst_ref=r3.at[b],
                send_sem=s3_s.at[b], recv_sem=s3_r.at[b],
                device_id=dev3, device_id_type=MESH,
            ).start()

        @pl.when(c >= LAG3)
        def _():
            b = c - LAG3
            wait_bytes(r3.at[b], s3_r.at[b])
            wg_ref[:, pl.ds(pl.multiple_of(b * DC, DC), DC)] = tot[b, zl] + r3[b]

        return 0

    lax.fori_loop(0, NC + LAG3, step, 0)

    wait_bytes(gate_in.at[pl.ds(0, NE - 1)], gr.at[0])
    wait_bytes(back_in.at[pl.ds(0, NE - 1)], ret_r.at[0])
    returned = unfold(back_in[...], FH)
    for k in range(2):
        gh_ref[k] = jnp.dot(picked[k], returned, preferred_element_type=F32).astype(BF16)
    shape = (NE, CAP, 128)
    diagonal = lax.broadcasted_iota(jnp.int32, shape, 1) == lax.broadcasted_iota(jnp.int32, shape, 2)
    column = jnp.sum(jnp.where(diagonal, gate_in[:, 0:1, :], 0.0), axis=2, keepdims=True).reshape(ROWS, 1)
    for k in range(2):
        value = jnp.sum(spots[k] * column, axis=0, keepdims=True)
        gg_ref[k : k + 1] = value / gates[k : k + 1]

    def settle(c, _):
        wait_bytes(send.at[c, pl.ds(0, NE - 1)], fwd_s.at[c])
        wait_bytes(part.at[c, pl.ds(0, 7)], s1_s.at[c])
        wait_bytes(q2.at[c, pl.ds(0, 7)], s2_s.at[c])
        wait_bytes(tot.at[c, 0], s3_s.at[c])
        return 0

    lax.fori_loop(0, NC, settle, 0)
    wait_bytes(back.at[pl.ds(0, NE - 1)], ret_s.at[0])
    wait_bytes(gate_out.at[pl.ds(0, NE - 1)], gs.at[0])


def body(grad_out, expert_ids, gate_probs, hidden_saved, w_down):
    vmem = pl.BlockSpec(memory_space=pltpu.VMEM)
    far = pl.BlockSpec(memory_space=pl.ANY)
    dma = pltpu.SemaphoreType.DMA
    gh, gg, wg = pl.pallas_call(
        kernel,
        out_shape=(
            jax.ShapeDtypeStruct((2, TOK, FF), BF16),
            jax.ShapeDtypeStruct((2, TOK), F32),
            jax.ShapeDtypeStruct((8, D), F32),
        ),
        in_specs=[vmem, vmem, vmem, far, far],
        out_specs=(vmem, vmem, vmem),
        scratch_shapes=[
            pltpu.VMEM((ROWS, FF), BF16),
            pltpu.VMEM((FF, D), BF16),
            pltpu.VMEM((ROWS, TOK), BF16),
            pltpu.VMEM((2, TOK, ROWS), BF16),
            pltpu.VMEM((FF, ROWS), BF16),
            pltpu.VMEM((NC, NE, 2 * CAP, H), BF16),
            pltpu.VMEM((NC, NE, 2 * CAP, H), BF16),
            pltpu.VMEM((ROWS, FF), F32),
            pltpu.VMEM((NC, 8, 96, DC), BF16),
            pltpu.VMEM((NC, 7, 96, DC), BF16),
            pltpu.VMEM((NC, 8, 16, DC), BF16),
            pltpu.VMEM((NC, 7, 16, DC), BF16),
            pltpu.VMEM((NC, 2, 8, DC), F32),
            pltpu.VMEM((NC, 8, DC), F32),
            pltpu.VMEM((NE, 2 * CAP, FH), BF16),
            pltpu.VMEM((NE, 2 * CAP, FH), BF16),
            pltpu.VMEM((NE, 8, 128), F32),
            pltpu.VMEM((NE, 8, 128), F32),
            dma((2,)),
            dma((NC,)), dma((NC,)), dma((NC,)), dma((NC,)),
            dma((NC,)), dma((NC,)), dma((NC,)), dma((NC,)),
            dma((1,)), dma((1,)), dma((1,)), dma((1,)),
        ],
        compiler_params=pltpu.CompilerParams(
            collective_id=0, has_side_effects=True, vmem_limit_bytes=48 * 2**20
        ),
        name="routed_backward",
    )(
        expert_ids.T,
        gate_probs.T,
        grad_out,
        hidden_saved.reshape(ROWS, FF),
        w_down.reshape(FF, D),
    )
    grad_hidden = jnp.transpose(gh, (1, 0, 2))
    grad_gate = gg.T.astype(BF16)
    return grad_hidden, grad_gate, wg[:6].reshape(1, 6, D)


def solution(mesh):
    in_specs = (
        P(("dp", "expert"), None),
        P(("dp", "expert"), None),
        P(("dp", "expert"), None),
        P("expert", "dp", None, None, None),
        P("expert", None, None),
    )
    out_specs = (
        P(("dp", "expert"), None, None),
        P(("dp", "expert"), None),
        P("expert", "dp", None),
    )
    return jax.shard_map(body, mesh=mesh, in_specs=in_specs, out_specs=out_specs, check_vma=False)
```

```python
import functools

import jax
import jax.numpy as jnp
from jax import lax
from jax.experimental import pallas as pl
from jax.experimental.pallas import tpu as pltpu
from jax.sharding import PartitionSpec as P

MESH = pl.DeviceIdType.MESH
NX, NY, NZ = 8, 8, 2
NE, CAP, TOK, D, FF = 8, 40, 128, 2048, 768
ROWS = NE * CAP
NC = 8
DC = D // NC
H = DC // 2
FH = FF // 2
NEAR, FAR = 2, 3
LAG1, LAG2, LAG3, LAG4 = 1, 3, 5, 8
F32, BF16 = jnp.float32, jnp.bfloat16
NT = (((1,), (1,)), ((), ()))


def wait_bytes(ref, sem):
    pltpu.make_async_copy(ref, ref, sem).wait()


def fold(block, width):
    left = block[:, :width].reshape(NE, CAP, width)
    right = block[:, width:].reshape(NE, CAP, width)
    return jnp.concatenate([left, right], axis=1).astype(BF16)


def unfold(block, width):
    block = block.astype(F32)
    left = block[:, :CAP, :].reshape(ROWS, width)
    right = block[:, CAP:, :].reshape(ROWS, width)
    return jnp.concatenate([left, right], axis=1).astype(BF16)


def kernel(
    ids_hbm, gate_hbm, go_hbm, hid_hbm, w_hbm,
    gh_ref, gg_ref, wg_ref,
    ids_ref, gate_ref, go_ref, hid, w, place, picked, hid_t, send, recv, grad, part, leaf, mid, r1, q2, r2, tot, r3,
    back, back_in, gate_out, gate_in,
    local, fwd_s, fwd_r, leaf_s, leaf_r, mid_s, s1_r, s2_s, s2_r, s3_s, s3_r, ret_s, ret_r, gs, gr,
):
    dp = lax.axis_index("dp")
    me = lax.axis_index("expert")
    core = lax.rem(me, 2)
    x, y, zl = dp // (NY * NZ), lax.rem(dp // NZ, NY), lax.rem(dp, NZ)
    first = jnp.where(core == 0, x, y)
    second = jnp.where(core == 0, y, x)

    def peer(k):
        return lax.rem(me + k, NE)

    def along(sx, sy):
        return (lax.rem(x + sx, NX) * NY + lax.rem(y + sy, NY)) * NZ + zl

    def dev1(k):
        k = lax.rem(jnp.int32(k), 8)
        return (along(k * (1 - core), k * core), me)

    def at(k):
        return lax.rem(first + k + 8, 8)

    def dev2(k):
        return (along(k * core, k * (1 - core)), me)

    dev3 = (dp + 1 - 2 * zl, me)

    barrier = pltpu.get_barrier_semaphore()

    def greet(k, _):
        for device in ((dp, peer(k)), dev2(k)):
            pl.semaphore_signal(barrier, inc=1, device_id=device, device_id_type=MESH)
        return 0

    lax.fori_loop(1, 8, greet, 0)
    for k in (1, 2, 6, 7):
        pl.semaphore_signal(barrier, inc=1, device_id=dev1(k), device_id_type=MESH)
    pl.semaphore_signal(barrier, inc=1, device_id=dev3, device_id_type=MESH)

    loads = [
        pltpu.make_async_copy(source, target, local.at[n])
        for n, (source, target) in enumerate(
            ((ids_hbm, ids_ref), (gate_hbm, gate_ref), (go_hbm, go_ref), (hid_hbm, hid), (w_hbm, w))
        )
    ]
    for load in loads:
        load.start()
    loads[0].wait()
    loads[1].wait()

    ids = ids_ref[...]
    gates = gate_ref[...].astype(F32)
    expert = lax.broadcasted_iota(jnp.int32, (NE, TOK), 0)
    chosen = [ids[k : k + 1] == expert for k in range(2)]
    named = jnp.where(chosen[0] | chosen[1], 1.0, 0.0)
    before = (
        lax.broadcasted_iota(jnp.int32, (TOK, TOK), 0) < lax.broadcasted_iota(jnp.int32, (TOK, TOK), 1)
    )
    slot = jnp.dot(
        named.astype(BF16), jnp.where(before, 1.0, 0.0).astype(BF16), preferred_element_type=F32
    )
    row = lax.broadcasted_iota(jnp.int32, (CAP, TOK), 0).astype(F32)
    spots = []
    for k in range(2):
        own = jnp.where(chosen[k], slot, -1.0)
        spots.append(
            jnp.concatenate(
                [jnp.where(row == own[e : e + 1], 1.0, 0.0) for e in range(NE)], axis=0
            )
        )
    place[...] = (spots[0] * gates[0:1] + spots[1] * gates[1:2]).astype(BF16)

    loads[2].wait()

    def dispatch(c):
        columns = go_ref[:, pl.ds(pl.multiple_of(c * DC, DC), DC)]
        rows = jnp.dot(place[...], columns, preferred_element_type=F32)
        send[c] = fold(rows, H)
        recv[c, me] = send[c, me]

    def forward(c, hops):
        for hop in hops:
            for other in range(2):
                if (hop, other) == (0, 0):
                    continue
                to = 2 * lax.rem(me // 2 + hop, 4) + lax.rem(core + other, 2)
                pltpu.make_async_remote_copy(
                    src_ref=send.at[c, to], dst_ref=recv.at[c, me],
                    send_sem=fwd_s.at[c], recv_sem=fwd_r.at[c],
                    device_id=(dp, to), device_id_type=MESH,
                ).start()

    dispatch(0)
    pl.semaphore_wait(barrier, 19)
    forward(0, (2,))
    forward(0, (1, 3, 0))

    def prepare(c, _):
        dispatch(c)

        @pl.when(c < FAR)
        def _():
            forward(c, (2,))

        @pl.when(c < NEAR)
        def _():
            forward(c, (1, 3, 0))

        return 0

    lax.fori_loop(1, NC, prepare, 0)

    eye = (
        lax.broadcasted_iota(jnp.int32, (TOK, TOK), 0) == lax.broadcasted_iota(jnp.int32, (TOK, TOK), 1)
    )
    eye = jnp.where(eye, 1.0, 0.0).astype(BF16)
    for k in range(2):
        picked[k] = lax.dot_general(
            eye, spots[k].astype(BF16), NT, preferred_element_type=F32
        ).astype(BF16)

    j = lax.broadcasted_iota(jnp.int32, (FF, 1), 0)
    major = (j * 683) >> 16
    rest = j - 96 * major
    minor = (rest * 171) >> 11
    turned = minor * 96 + major * 12 + (rest - 12 * minor)
    source = jnp.where(core == 0, j, turned)
    order = jnp.where(lax.broadcasted_iota(jnp.int32, (FF, FF), 1) == source, 1.0, 0.0).astype(BF16)
    loads[3].wait()
    hid_t[...] = lax.dot_general(order, hid[...], NT, preferred_element_type=F32).astype(BF16)
    grad[...] = jnp.zeros_like(grad)

    i = lax.broadcasted_iota(jnp.int32, (128, 1), 0)
    inner = i & 7
    origin = (i >> 4) * 12 + ((i >> 3) & 1) * 6 + inner
    spread = lax.broadcasted_iota(jnp.int32, (128, 96), 1) == jnp.where(inner < 6, origin, -1)
    spread = jnp.where(spread, 1.0, 0.0).astype(BF16)
    loads[4].wait()

    def step(c, _):
        @pl.when(c < NC)
        def _():
            wait_bytes(recv.at[c, pl.ds(0, NE - 1)], fwd_r.at[c])

            @pl.when(c + FAR < NC)
            def _():
                forward(c + FAR, (2,))

            @pl.when(c + NEAR < NC)
            def _():
                forward(c + NEAR, (1, 3, 0))

            rows = unfold(recv[c], H)
            part[c] = (
                jnp.dot(hid_t[...], rows, preferred_element_type=F32).astype(BF16).reshape(8, 96, DC)
            )

            sign = 1 - 2 * lax.rem(c, 2)
            for owner, via, target in (
                (-4, -2, leaf.at[c, 0]), (-3, -1, leaf.at[c, 1]), (3, 1, leaf.at[c, 2]),
                (-1, -1, r1.at[c, 0]), (1, 1, r1.at[c, 1]),
            ):
                pltpu.make_async_remote_copy(
                    src_ref=part.at[c, at(sign * owner)], dst_ref=target, send_sem=leaf_s.at[c],
                    recv_sem=s1_r.at[c] if abs(owner) == 1 else leaf_r.at[c],
                    device_id=dev1(sign * via + 8), device_id_type=MESH,
                ).start()
            columns = w[:, pl.ds(pl.multiple_of(c * DC, DC), DC)]
            grad[...] += lax.dot_general(rows, columns, NT, preferred_element_type=F32)

            @pl.when(c == NC - 1)
            def _():
                back[...] = fold(grad[...], FH)
                back_in[me] = back[me]

                def one(k, _):
                    pltpu.make_async_remote_copy(
                        src_ref=back.at[peer(k)], dst_ref=back_in.at[me],
                        send_sem=ret_s.at[0], recv_sem=ret_r.at[0],
                        device_id=(dp, peer(k)), device_id_type=MESH,
                    ).start()
                    return 0

                lax.fori_loop(1, NE, one, 0)
        @pl.when(c == NC - 1)
        def _():
            total = grad[...]
            gate_sum = jnp.sum(hid[...].astype(F32) * total, axis=1, keepdims=True)
            shape = (NE, CAP, 128)
            diagonal = lax.broadcasted_iota(jnp.int32, shape, 1) == lax.broadcasted_iota(jnp.int32, shape, 2)
            flat = jnp.sum(
                jnp.where(diagonal, gate_sum.reshape(NE, CAP, 1), 0.0), axis=1, keepdims=True
            )
            gate_out[...] = jnp.broadcast_to(flat, (NE, 8, 128))
            gate_in[me] = gate_out[me]

            def one(k, _):
                pltpu.make_async_remote_copy(
                    src_ref=gate_out.at[peer(k)], dst_ref=gate_in.at[me],
                    send_sem=gs.at[0], recv_sem=gr.at[0],
                    device_id=(dp, peer(k)), device_id_type=MESH,
                ).start()
                return 0

            lax.fori_loop(1, NE, one, 0)

        @pl.when((c >= LAG1) & (c < NC + LAG1))
        def _():
            b = c - LAG1
            sign = 1 - 2 * lax.rem(b, 2)
            wait_bytes(leaf.at[b], leaf_r.at[b])
            far_side = part[b, at(-2 * sign)].astype(F32) + leaf[b, 0].astype(F32) + leaf[b, 1].astype(F32)
            near_side = part[b, at(2 * sign)].astype(F32) + leaf[b, 2].astype(F32)
            mid[b, 0] = far_side.astype(BF16)
            mid[b, 1] = near_side.astype(BF16)
            for n, owner in enumerate((-2, 2)):
                pltpu.make_async_remote_copy(
                    src_ref=mid.at[b, n], dst_ref=r1.at[b, 2 + n],
                    send_sem=mid_s.at[b], recv_sem=s1_r.at[b],
                    device_id=dev1(sign * owner + 8), device_id_type=MESH,
                ).start()

        @pl.when((c >= LAG2) & (c < NC + LAG2))
        def _():
            b = c - LAG2
            wait_bytes(r1.at[b], s1_r.at[b])
            total = part[b, first].astype(F32)
            for k in range(4):
                total += r1[b, k].astype(F32)
            wide = jnp.dot(spread, total.astype(BF16), preferred_element_type=F32)
            q2[b] = wide.astype(BF16).reshape(8, 16, DC)

            def one(k, _):
                pltpu.make_async_remote_copy(
                    src_ref=q2.at[b, lax.rem(second + k, 8)], dst_ref=r2.at[b, k - 1],
                    send_sem=s2_s.at[b], recv_sem=s2_r.at[b],
                    device_id=dev2(k), device_id_type=MESH,
                ).start()
                return 0

            lax.fori_loop(1, 8, one, 0)

        @pl.when((c >= LAG3) & (c < NC + LAG3))
        def _():
            b = c - LAG3
            wait_bytes(r2.at[b], s2_r.at[b])
            total = q2[b, second].astype(F32)
            for k in range(7):
                total += r2[b, k].astype(F32)
            tot[b] = total.reshape(2, 8, DC)
            pltpu.make_async_remote_copy(
                src_ref=tot.at[b, 1 - zl], dst_ref=r3.at[b],
                send_sem=s3_s.at[b], recv_sem=s3_r.at[b],
                device_id=dev3, device_id_type=MESH,
            ).start()

        @pl.when(c >= LAG4)
        def _():
            b = c - LAG4
            wait_bytes(r3.at[b], s3_r.at[b])
            wg_ref[:, pl.ds(pl.multiple_of(b * DC, DC), DC)] = tot[b, zl] + r3[b]

        return 0

    lax.fori_loop(0, NC + LAG4, step, 0)

    wait_bytes(gate_in.at[pl.ds(0, NE - 1)], gr.at[0])
    wait_bytes(back_in.at[pl.ds(0, NE - 1)], ret_r.at[0])
    returned = unfold(back_in[...], FH)
    for k in range(2):
        gh_ref[k] = jnp.dot(picked[k], returned, preferred_element_type=F32).astype(BF16)
    shape = (NE, CAP, 128)
    diagonal = lax.broadcasted_iota(jnp.int32, shape, 1) == lax.broadcasted_iota(jnp.int32, shape, 2)
    column = jnp.sum(jnp.where(diagonal, gate_in[:, 0:1, :], 0.0), axis=2, keepdims=True).reshape(ROWS, 1)
    for k in range(2):
        value = jnp.sum(spots[k] * column, axis=0, keepdims=True)
        gg_ref[k : k + 1] = value / gates[k : k + 1]

    def settle(c, _):
        wait_bytes(send.at[c, pl.ds(0, NE - 1)], fwd_s.at[c])
        wait_bytes(part.at[c, pl.ds(0, 5)], leaf_s.at[c])
        wait_bytes(mid.at[c], mid_s.at[c])
        wait_bytes(q2.at[c, pl.ds(0, 7)], s2_s.at[c])
        wait_bytes(tot.at[c, 0], s3_s.at[c])
        return 0

    lax.fori_loop(0, NC, settle, 0)
    wait_bytes(back.at[pl.ds(0, NE - 1)], ret_s.at[0])
    wait_bytes(gate_out.at[pl.ds(0, NE - 1)], gs.at[0])


def body(grad_out, expert_ids, gate_probs, hidden_saved, w_down):
    vmem = pl.BlockSpec(memory_space=pltpu.VMEM)
    far = pl.BlockSpec(memory_space=pltpu.HBM)
    dma = pltpu.SemaphoreType.DMA
    gh, gg, wg = pl.pallas_call(
        kernel,
        out_shape=(
            jax.ShapeDtypeStruct((2, TOK, FF), BF16),
            jax.ShapeDtypeStruct((2, TOK), F32),
            jax.ShapeDtypeStruct((8, D), F32),
        ),
        in_specs=[far] * 5,
        out_specs=(vmem, vmem, vmem),
        scratch_shapes=[
            pltpu.VMEM((2, TOK), jnp.int32),
            pltpu.VMEM((2, TOK), BF16),
            pltpu.VMEM((TOK, D), BF16),
            pltpu.VMEM((ROWS, FF), BF16),
            pltpu.VMEM((FF, D), BF16),
            pltpu.VMEM((ROWS, TOK), BF16),
            pltpu.VMEM((2, TOK, ROWS), BF16),
            pltpu.VMEM((FF, ROWS), BF16),
            pltpu.VMEM((NC, NE, 2 * CAP, H), BF16),
            pltpu.VMEM((NC, NE, 2 * CAP, H), BF16),
            pltpu.VMEM((ROWS, FF), F32),
            pltpu.VMEM((NC, 8, 96, DC), BF16),
            pltpu.VMEM((NC, 3, 96, DC), BF16),
            pltpu.VMEM((NC, 2, 96, DC), BF16),
            pltpu.VMEM((NC, 4, 96, DC), BF16),
            pltpu.VMEM((NC, 8, 16, DC), BF16),
            pltpu.VMEM((NC, 7, 16, DC), BF16),
            pltpu.VMEM((NC, 2, 8, DC), F32),
            pltpu.VMEM((NC, 8, DC), F32),
            pltpu.VMEM((NE, 2 * CAP, FH), BF16),
            pltpu.VMEM((NE, 2 * CAP, FH), BF16),
            pltpu.VMEM((NE, 8, 128), F32),
            pltpu.VMEM((NE, 8, 128), F32),
            dma((5,)),
            *[dma((NC,))] * 10,
            dma((1,)), dma((1,)), dma((1,)), dma((1,)),
        ],
        compiler_params=pltpu.CompilerParams(
            collective_id=0, has_side_effects=True, vmem_limit_bytes=533 * 2**20 // 10
        ),
        name="routed_backward",
    )(
        expert_ids.T,
        gate_probs.T,
        grad_out,
        hidden_saved.reshape(ROWS, FF),
        w_down.reshape(FF, D),
    )
    grad_hidden = jnp.transpose(gh, (1, 0, 2))
    grad_gate = gg.T.astype(BF16)
    return grad_hidden, grad_gate, wg[:6].reshape(1, 6, D)


def solution(mesh):
    in_specs = (
        P(("dp", "expert"), None),
        P(("dp", "expert"), None),
        P(("dp", "expert"), None),
        P("expert", "dp", None, None, None),
        P("expert", None, None),
    )
    out_specs = (
        P(("dp", "expert"), None, None),
        P(("dp", "expert"), None),
        P("expert", "dp", None),
    )
    return jax.shard_map(body, mesh=mesh, in_specs=in_specs, out_specs=out_specs, check_vma=False)
```

```python
import functools

import jax
import jax.numpy as jnp
from jax import lax
from jax.experimental import pallas as pl
from jax.experimental.pallas import tpu as pltpu
from jax.sharding import PartitionSpec as P

MESH = pl.DeviceIdType.MESH
NX, NY, NZ = 8, 8, 2
NE, CAP, TOK, D, FF = 8, 40, 128, 2048, 768
ROWS = NE * CAP
NC = 8
DC = D // NC
H = DC // 2
FH = FF // 2
NEAR, FAR = 2, 2
LAG1, LAG2, LAG3, LAG4 = 1, 3, 5, 8
F32, BF16 = jnp.float32, jnp.bfloat16
NT = (((1,), (1,)), ((), ()))


def wait_bytes(ref, sem):
    pltpu.make_async_copy(ref, ref, sem).wait()


def fold(block, width):
    left = block[:, :width].reshape(NE, CAP, width)
    right = block[:, width:].reshape(NE, CAP, width)
    return jnp.concatenate([left, right], axis=1).astype(BF16)


def unfold(block, width):
    block = block.astype(F32)
    left = block[:, :CAP, :].reshape(ROWS, width)
    right = block[:, CAP:, :].reshape(ROWS, width)
    return jnp.concatenate([left, right], axis=1).astype(BF16)


def kernel(
    ids_hbm, gate_hbm, go_hbm, hid_hbm, w_hbm,
    gh_ref, gg_ref, wg_ref,
    ids_ref, gate_ref, go_ref, hid, w, place, picked, hid_t, send, recv, grad, part, leaf, mid, r1, q2, r2, tot, r3,
    back, back_in, gate_out, gate_in,
    local, fwd_s, fwd_r, leaf_s, leaf_r, mid_s, s1_r, s2_s, s2_r, s3_s, s3_r, ret_s, ret_r, gs, gr,
):
    dp = lax.axis_index("dp")
    me = lax.axis_index("expert")
    core = lax.rem(me, 2)
    x, y, zl = dp // (NY * NZ), lax.rem(dp // NZ, NY), lax.rem(dp, NZ)
    first = jnp.where(core == 0, x, y)
    second = jnp.where(core == 0, y, x)

    def peer(k):
        return lax.rem(me + k, NE)

    def along(sx, sy):
        return (lax.rem(x + sx, NX) * NY + lax.rem(y + sy, NY)) * NZ + zl

    def dev1(k):
        k = lax.rem(jnp.int32(k), 8)
        return (along(k * (1 - core), k * core), me)

    def at(k):
        return lax.rem(first + k + 8, 8)

    def dev2(k):
        return (along(k * core, k * (1 - core)), me)

    dev3 = (dp + 1 - 2 * zl, me)

    barrier = pltpu.get_barrier_semaphore()

    def greet(k, _):
        for device in ((dp, peer(k)), dev2(k)):
            pl.semaphore_signal(barrier, inc=1, device_id=device, device_id_type=MESH)
        return 0

    lax.fori_loop(1, 8, greet, 0)
    for k in (1, 2, 6, 7):
        pl.semaphore_signal(barrier, inc=1, device_id=dev1(k), device_id_type=MESH)
    pl.semaphore_signal(barrier, inc=1, device_id=dev3, device_id_type=MESH)

    loads = [
        pltpu.make_async_copy(source, target, local.at[n])
        for n, (source, target) in enumerate(
            ((ids_hbm, ids_ref), (gate_hbm, gate_ref), (go_hbm, go_ref), (hid_hbm, hid), (w_hbm, w))
        )
    ]
    for load in loads:
        load.start()
    loads[0].wait()
    loads[1].wait()

    ids = ids_ref[...]
    gates = gate_ref[...].astype(F32)
    expert = lax.broadcasted_iota(jnp.int32, (NE, TOK), 0)
    chosen = [ids[k : k + 1] == expert for k in range(2)]
    named = jnp.where(chosen[0] | chosen[1], 1.0, 0.0)
    before = (
        lax.broadcasted_iota(jnp.int32, (TOK, TOK), 0) < lax.broadcasted_iota(jnp.int32, (TOK, TOK), 1)
    )
    slot = jnp.dot(
        named.astype(BF16), jnp.where(before, 1.0, 0.0).astype(BF16), preferred_element_type=F32
    )
    row = lax.broadcasted_iota(jnp.int32, (CAP, TOK), 0).astype(F32)
    spots = []
    for k in range(2):
        own = jnp.where(chosen[k], slot, -1.0)
        spots.append(
            jnp.concatenate(
                [jnp.where(row == own[e : e + 1], 1.0, 0.0) for e in range(NE)], axis=0
            )
        )
    place[...] = (spots[0] * gates[0:1] + spots[1] * gates[1:2]).astype(BF16)

    loads[2].wait()

    def dispatch(c):
        columns = go_ref[:, pl.ds(pl.multiple_of(c * DC, DC), DC)]
        rows = jnp.dot(place[...], columns, preferred_element_type=F32)
        send[c] = fold(rows, H)
        recv[c, me] = send[c, me]

    def forward(c, hops):
        for hop in hops:
            for other in range(2):
                if (hop, other) == (0, 0):
                    continue
                to = 2 * lax.rem(me // 2 + hop, 4) + lax.rem(core + other, 2)
                pltpu.make_async_remote_copy(
                    src_ref=send.at[c, to], dst_ref=recv.at[c, me],
                    send_sem=fwd_s.at[c], recv_sem=fwd_r.at[c],
                    device_id=(dp, to), device_id_type=MESH,
                ).start()

    dispatch(0)
    pl.semaphore_wait(barrier, 19)
    forward(0, (2,))
    forward(0, (1, 3, 0))

    def prepare(c, _):
        dispatch(c)

        forward(c, (2,))

        @pl.when(c < NEAR)
        def _():
            forward(c, (1, 3, 0))

        return 0

    lax.fori_loop(1, FAR, prepare, 0)

    j = lax.broadcasted_iota(jnp.int32, (FF, 1), 0)
    major = (j * 683) >> 16
    rest = j - 96 * major
    minor = (rest * 171) >> 11
    turned = minor * 96 + major * 12 + (rest - 12 * minor)
    source = jnp.where(core == 0, j, turned)
    order = jnp.where(lax.broadcasted_iota(jnp.int32, (FF, FF), 1) == source, 1.0, 0.0).astype(BF16)
    loads[3].wait()
    hid_t[...] = lax.dot_general(order, hid[...], NT, preferred_element_type=F32).astype(BF16)
    grad[...] = jnp.zeros_like(grad)

    i = lax.broadcasted_iota(jnp.int32, (128, 1), 0)
    inner = i & 7
    origin = (i >> 4) * 12 + ((i >> 3) & 1) * 6 + inner
    spread = lax.broadcasted_iota(jnp.int32, (128, 96), 1) == jnp.where(inner < 6, origin, -1)
    spread = jnp.where(spread, 1.0, 0.0).astype(BF16)
    loads[4].wait()

    def step(c, _):
        @pl.when(c < NC)
        def _():
            @pl.when(c + FAR < NC)
            def _():
                dispatch(c + FAR)

            wait_bytes(recv.at[c, pl.ds(0, NE - 1)], fwd_r.at[c])

            @pl.when(c + FAR < NC)
            def _():
                forward(c + FAR, (2,))

            @pl.when(c + NEAR < NC)
            def _():
                forward(c + NEAR, (1, 3, 0))

            rows = unfold(recv[c], H)
            part[c] = (
                jnp.dot(hid_t[...], rows, preferred_element_type=F32).astype(BF16).reshape(8, 96, DC)
            )

            sign = 1 - 2 * lax.rem(c, 2)
            for owner, via, target in (
                (-4, -2, leaf.at[c, 0]), (-3, -1, leaf.at[c, 1]), (3, 1, leaf.at[c, 2]),
                (-1, -1, r1.at[c, 0]), (1, 1, r1.at[c, 1]),
            ):
                pltpu.make_async_remote_copy(
                    src_ref=part.at[c, at(sign * owner)], dst_ref=target, send_sem=leaf_s.at[c],
                    recv_sem=s1_r.at[c] if abs(owner) == 1 else leaf_r.at[c],
                    device_id=dev1(sign * via + 8), device_id_type=MESH,
                ).start()
            columns = w[:, pl.ds(pl.multiple_of(c * DC, DC), DC)]
            grad[...] += lax.dot_general(rows, columns, NT, preferred_element_type=F32)

            @pl.when(c == NC - 1)
            def _():
                back[...] = fold(grad[...], FH)
                back_in[me] = back[me]

                def one(k, _):
                    pltpu.make_async_remote_copy(
                        src_ref=back.at[peer(k)], dst_ref=back_in.at[me],
                        send_sem=ret_s.at[0], recv_sem=ret_r.at[0],
                        device_id=(dp, peer(k)), device_id_type=MESH,
                    ).start()
                    return 0

                lax.fori_loop(1, NE, one, 0)
        @pl.when(c == NC - 1)
        def _():
            total = grad[...]
            gate_sum = jnp.sum(hid[...].astype(F32) * total, axis=1, keepdims=True)
            shape = (NE, CAP, 128)
            diagonal = lax.broadcasted_iota(jnp.int32, shape, 1) == lax.broadcasted_iota(jnp.int32, shape, 2)
            flat = jnp.sum(
                jnp.where(diagonal, gate_sum.reshape(NE, CAP, 1), 0.0), axis=1, keepdims=True
            )
            gate_out[...] = jnp.broadcast_to(flat, (NE, 8, 128))
            gate_in[me] = gate_out[me]

            def one(k, _):
                pltpu.make_async_remote_copy(
                    src_ref=gate_out.at[peer(k)], dst_ref=gate_in.at[me],
                    send_sem=gs.at[0], recv_sem=gr.at[0],
                    device_id=(dp, peer(k)), device_id_type=MESH,
                ).start()
                return 0

            lax.fori_loop(1, NE, one, 0)

        @pl.when((c >= LAG1) & (c < NC + LAG1))
        def _():
            b = c - LAG1
            sign = 1 - 2 * lax.rem(b, 2)
            wait_bytes(leaf.at[b], leaf_r.at[b])
            far_side = part[b, at(-2 * sign)].astype(F32) + leaf[b, 0].astype(F32) + leaf[b, 1].astype(F32)
            near_side = part[b, at(2 * sign)].astype(F32) + leaf[b, 2].astype(F32)
            mid[b, 0] = far_side.astype(BF16)
            mid[b, 1] = near_side.astype(BF16)
            for n, owner in enumerate((-2, 2)):
                pltpu.make_async_remote_copy(
                    src_ref=mid.at[b, n], dst_ref=r1.at[b, 2 + n],
                    send_sem=mid_s.at[b], recv_sem=s1_r.at[b],
                    device_id=dev1(sign * owner + 8), device_id_type=MESH,
                ).start()

        @pl.when((c >= LAG2) & (c < NC + LAG2))
        def _():
            b = c - LAG2
            wait_bytes(r1.at[b], s1_r.at[b])
            total = part[b, first].astype(F32)
            for k in range(4):
                total += r1[b, k].astype(F32)
            wide = jnp.dot(spread, total.astype(BF16), preferred_element_type=F32)
            q2[b] = wide.astype(BF16).reshape(8, 16, DC)

            def one(k, _):
                pltpu.make_async_remote_copy(
                    src_ref=q2.at[b, lax.rem(second + k, 8)], dst_ref=r2.at[b, k - 1],
                    send_sem=s2_s.at[b], recv_sem=s2_r.at[b],
                    device_id=dev2(k), device_id_type=MESH,
                ).start()
                return 0

            lax.fori_loop(1, 8, one, 0)

        @pl.when((c >= LAG3) & (c < NC + LAG3))
        def _():
            b = c - LAG3
            wait_bytes(r2.at[b], s2_r.at[b])
            total = q2[b, second].astype(F32)
            for k in range(7):
                total += r2[b, k].astype(F32)
            tot[b] = total.reshape(2, 8, DC)
            pltpu.make_async_remote_copy(
                src_ref=tot.at[b, 1 - zl], dst_ref=r3.at[b],
                send_sem=s3_s.at[b], recv_sem=s3_r.at[b],
                device_id=dev3, device_id_type=MESH,
            ).start()

        @pl.when(c >= LAG4)
        def _():
            b = c - LAG4
            wait_bytes(r3.at[b], s3_r.at[b])
            wg_ref[:, pl.ds(pl.multiple_of(b * DC, DC), DC)] = tot[b, zl] + r3[b]

        @pl.when(c == 2)
        def _():
            eye = (
                lax.broadcasted_iota(jnp.int32, (TOK, TOK), 0)
                == lax.broadcasted_iota(jnp.int32, (TOK, TOK), 1)
            )
            eye = jnp.where(eye, 1.0, 0.0).astype(BF16)
            for k in range(2):
                picked[k] = lax.dot_general(
                    eye, spots[k].astype(BF16), NT, preferred_element_type=F32
                ).astype(BF16)

        return 0

    lax.fori_loop(0, NC + LAG4, step, 0)

    wait_bytes(gate_in.at[pl.ds(0, NE - 1)], gr.at[0])
    wait_bytes(back_in.at[pl.ds(0, NE - 1)], ret_r.at[0])
    returned = unfold(back_in[...], FH)
    for k in range(2):
        gh_ref[k] = jnp.dot(picked[k], returned, preferred_element_type=F32).astype(BF16)
    shape = (NE, CAP, 128)
    diagonal = lax.broadcasted_iota(jnp.int32, shape, 1) == lax.broadcasted_iota(jnp.int32, shape, 2)
    column = jnp.sum(jnp.where(diagonal, gate_in[:, 0:1, :], 0.0), axis=2, keepdims=True).reshape(ROWS, 1)
    for k in range(2):
        value = jnp.sum(spots[k] * column, axis=0, keepdims=True)
        gg_ref[k : k + 1] = value / gates[k : k + 1]

    def settle(c, _):
        wait_bytes(send.at[c, pl.ds(0, NE - 1)], fwd_s.at[c])
        wait_bytes(part.at[c, pl.ds(0, 5)], leaf_s.at[c])
        wait_bytes(mid.at[c], mid_s.at[c])
        wait_bytes(q2.at[c, pl.ds(0, 7)], s2_s.at[c])
        wait_bytes(tot.at[c, 0], s3_s.at[c])
        return 0

    lax.fori_loop(0, NC, settle, 0)
    wait_bytes(back.at[pl.ds(0, NE - 1)], ret_s.at[0])
    wait_bytes(gate_out.at[pl.ds(0, NE - 1)], gs.at[0])


def body(grad_out, expert_ids, gate_probs, hidden_saved, w_down):
    vmem = pl.BlockSpec(memory_space=pltpu.VMEM)
    far = pl.BlockSpec(memory_space=pltpu.HBM)
    dma = pltpu.SemaphoreType.DMA
    gh, gg, wg = pl.pallas_call(
        kernel,
        out_shape=(
            jax.ShapeDtypeStruct((2, TOK, FF), BF16),
            jax.ShapeDtypeStruct((2, TOK), F32),
            jax.ShapeDtypeStruct((8, D), F32),
        ),
        in_specs=[far] * 5,
        out_specs=(vmem, vmem, vmem),
        scratch_shapes=[
            pltpu.VMEM((2, TOK), jnp.int32),
            pltpu.VMEM((2, TOK), BF16),
            pltpu.VMEM((TOK, D), BF16),
            pltpu.VMEM((ROWS, FF), BF16),
            pltpu.VMEM((FF, D), BF16),
            pltpu.VMEM((ROWS, TOK), BF16),
            pltpu.VMEM((2, TOK, ROWS), BF16),
            pltpu.VMEM((FF, ROWS), BF16),
            pltpu.VMEM((NC, NE, 2 * CAP, H), BF16),
            pltpu.VMEM((NC, NE, 2 * CAP, H), BF16),
            pltpu.VMEM((ROWS, FF), F32),
            pltpu.VMEM((NC, 8, 96, DC), BF16),
            pltpu.VMEM((NC, 3, 96, DC), BF16),
            pltpu.VMEM((NC, 2, 96, DC), BF16),
            pltpu.VMEM((NC, 4, 96, DC), BF16),
            pltpu.VMEM((NC, 8, 16, DC), BF16),
            pltpu.VMEM((NC, 7, 16, DC), BF16),
            pltpu.VMEM((NC, 2, 8, DC), F32),
            pltpu.VMEM((NC, 8, DC), F32),
            pltpu.VMEM((NE, 2 * CAP, FH), BF16),
            pltpu.VMEM((NE, 2 * CAP, FH), BF16),
            pltpu.VMEM((NE, 8, 128), F32),
            pltpu.VMEM((NE, 8, 128), F32),
            dma((5,)),
            *[dma((NC,))] * 10,
            dma((1,)), dma((1,)), dma((1,)), dma((1,)),
        ],
        compiler_params=pltpu.CompilerParams(
            collective_id=0, has_side_effects=True, vmem_limit_bytes=533 * 2**20 // 10
        ),
        name="routed_backward",
    )(
        expert_ids.T,
        gate_probs.T,
        grad_out,
        hidden_saved.reshape(ROWS, FF),
        w_down.reshape(FF, D),
    )
    grad_hidden = jnp.transpose(gh, (1, 0, 2))
    grad_gate = gg.T.astype(BF16)
    return grad_hidden, grad_gate, wg[:6].reshape(1, 6, D)


def solution(mesh):
    in_specs = (
        P(("dp", "expert"), None),
        P(("dp", "expert"), None),
        P(("dp", "expert"), None),
        P("expert", "dp", None, None, None),
        P("expert", None, None),
    )
    out_specs = (
        P(("dp", "expert"), None, None),
        P(("dp", "expert"), None),
        P("expert", "dp", None),
    )
    return jax.shard_map(body, mesh=mesh, in_specs=in_specs, out_specs=out_specs, check_vma=False)
```
